32 devices in a mesh: shard: 4 (over z), rep: 8 (over y, x, core).
Axes of the slice: x: 2, y: 2, z: 4, core: 2. Of those that a mesh axis runs over, the one named last changes fastest.
Arguments:
- latents_in: bfloat16 [65536, 384], P(('shard', 'rep')), may hold values from -6 to 6
- conditioning: bfloat16 [256, 384], P(('shard', 'rep')), may hold values from -6 to 6
- ada_weight: bfloat16 [384, 2304], P('shard'), may hold values from -0.3125 to 0.3125
- ada_bias: bfloat16 [2304], P('shard'), may hold values from -1.796875 to 1.796875
- qkv_weight: bfloat16 [384, 1152], P('shard'), may hold values from -0.3125 to 0.3125
- qv_bias: bfloat16 [768], P('shard'), may hold values from -1.796875 to 1.796875
- proj_weight: bfloat16 [384, 384], P('shard'), may hold values from -1.25 to 1.25
- proj_bias: bfloat16 [384], P('shard'), may hold values from -1.796875 to 1.796875
- fc1_weight: bfloat16 [384, 1536], P('shard'), may hold values from -0.3125 to 0.3125
- fc1_bias: bfloat16 [1536], P('shard'), may hold values from -1.796875 to 1.796875
- fc2_weight: bfloat16 [1536, 384], P('shard'), may hold values from -0.15625 to 0.15625
- fc2_bias: bfloat16 [384], P('shard'), may hold values from -1.796875 to 1.796875
- cotangent: bfloat16 [65536, 384], P(('shard', 'rep')), may hold values from -6 to 6
Outputs:
- layer_out: bfloat16 [65536, 384], P(('shard', 'rep'))
- grad_latents: float32 [65536, 384], P(('shard', 'rep'))
- grad_conditioning: float32 [256, 384], P(('shard', 'rep'))
- grad_ada_weight: float32 [384, 2304], P('shard')
- grad_ada_bias: float32 [2304], P('shard')
- grad_qkv_weight: float32 [384, 1152], P('shard')
- grad_qv_bias: float32 [768], P('shard')
- grad_proj_weight: float32 [384, 384], P('shard')
- grad_proj_bias: float32 [384], P('shard')
- grad_fc1_weight: float32 [384, 1536], P('shard')
- grad_fc1_bias: float32 [1536], P('shard')
- grad_fc2_weight: float32 [1536, 384], P('shard')
- grad_fc2_bias: float32 [384], P('shard')
The draws below stay inside these ranges and needn't reach their ends.
All inputs are finite; a program needn't handle non-finite values.
Results may differ from the reference program's by a relative error of at most 0.01.
The reference program's roundings to bfloat16 on the way count: a program that leaves them out, or rounds other values in their place, can miss the bound.
Values may be sent and summed in bfloat16 or wider, within the bound.
A program may use at most 128 MiB of HBM per device.

```python
import jax
import jax.numpy as jnp
from jax import lax

D = 384
HEAD_DIM = 64
FF = 1536
SEQ = 256
LAT_DEV = 8
LATENTS = 256
TOKENS = 65536


def steps_of(key, extent, pieces, low, largest):
    level = 1.0
    for axis_at, parts in pieces:
        draws = jax.random.uniform(jax.random.fold_in(jax.random.fold_in(key, 6), axis_at), (parts,), jnp.float32, low / len(pieces), largest / len(pieces))
        level = level * jnp.repeat(jnp.exp(draws), extent[axis_at] // parts).reshape((-1,) + (1,) * (len(extent) - 1 - axis_at))
    return level


def bell_draw(stream_key, shape, scale, reach, pieces=(), held_as=jnp.bfloat16):
    result = jax.random.normal(stream_key, shape, jnp.float32) * scale
    if len(pieces) > 0:
        result = steps_of(stream_key, shape, pieces, -0.22, 0.18) * result
    return jnp.clip(result, min=-reach, max=reach).astype(held_as)


def setup_inputs(seed: int = 0) -> dict:
    seeds = jax.random.split(jax.random.key(seed), 14)
    return {
        "latents_in": bell_draw(seeds[0], (TOKENS, D), 1.0, 6.0, ((0, 32),)),
        "conditioning": bell_draw(seeds[1], (LATENTS, D), 1.0, 6.0, ((0, 32),)),
        "ada_weight": bell_draw(seeds[2], (D, 6 * D), D ** -0.5, 0.3125, ((0, 4),)),
        "ada_bias": bell_draw(seeds[3], (6 * D,), 0.3, 1.796875, ((0, 4),)),
        "qkv_weight": bell_draw(seeds[4], (D, 3 * D), D ** -0.5, 0.3125, ((0, 4),)),
        "qv_bias": bell_draw(seeds[5], (2 * D,), 0.3, 1.796875, ((0, 4),)),
        "proj_weight": bell_draw(seeds[6], (D, D), (D // 16) ** -0.5, 1.25, ((0, 4),)),
        "proj_bias": bell_draw(seeds[7], (D,), 0.3, 1.796875, ((0, 4),)),
        "fc1_weight": bell_draw(seeds[8], (D, FF), D ** -0.5, 0.3125, ((0, 4),)),
        "fc1_bias": bell_draw(seeds[9], (FF,), 0.3, 1.796875, ((0, 4),)),
        "fc2_weight": bell_draw(seeds[10], (FF, D), FF ** -0.5, 0.15625, ((0, 4),)),
        "fc2_bias": bell_draw(seeds[11], (D,), 0.3, 1.796875, ((0, 4),)),
        "cotangent": bell_draw(seeds[12], (TOKENS, D), 1.0, 6.0, ((0, 32),)),
    }


EPSILON = 1e-06
HIGH = lax.Precision.HIGHEST

@jax.custom_vjp
def low(v):
    return lax.optimization_barrier(v.astype(jnp.bfloat16)).astype(jnp.float32)

@jax.custom_vjp
def low_back(v):
    return v

def low_keep(v):
    return (low(v), None)

def low_pass(kept, grad):
    return (grad,)

def back_keep(v):
    return (v, None)

def back_low(kept, grad):
    return (low(grad),)
low.defvjp(low_keep, low_pass)
low_back.defvjp(back_keep, back_low)

def layer_norm(values):
    center = values - lax.optimization_barrier(jnp.mean(values, axis=-1, keepdims=True))
    spread = lax.optimization_barrier(jnp.mean(center * center, axis=-1, keepdims=True))
    return center * lax.rsqrt(spread + EPSILON)

def modulate(values, shift_rows, scale_rows):
    return layer_norm(values) * (1.0 + scale_rows[:, None, :]) + shift_rows[:, None, :]

def project(inputs, weight):
    return jnp.einsum('lsd,de->lse', inputs, weight, precision=HIGH)

def layer(inputs, cond_rows, ada_weight, ada_bias, qkv_weight, qv_bias, proj_weight, proj_bias, fc1_weight, fc1_bias, fc2_weight, fc2_bias):
    latent_count, seq_length, model_width = inputs.shape
    head_count = model_width // HEAD_DIM
    silu_low = low(jax.nn.silu(cond_rows))
    modulation = low_back(jnp.dot(silu_low, ada_weight, precision=HIGH) + ada_bias)
    shift_one, scale_one, gate_one, shift_two, scale_two, gate_two = jnp.split(modulation, 6, axis=1)
    first_low = low(modulate(inputs, shift_one, scale_one))
    full_bias = jnp.concatenate([qv_bias[:model_width], jnp.zeros((model_width,), inputs.dtype), qv_bias[model_width:]])
    qkv_low = low(low_back(project(first_low, qkv_weight) + full_bias))
    qkv_low = qkv_low.reshape(latent_count, seq_length, 3, head_count, HEAD_DIM)
    queries = qkv_low[:, :, 0]
    key_rows = qkv_low[:, :, 1]
    value_rows = qkv_low[:, :, 2]
    scores = low_back(jnp.einsum('lqhd,lkhd->lhqk', queries, key_rows, precision=HIGH) * HEAD_DIM ** (-0.5))
    row_max = lax.optimization_barrier(jnp.max(scores, axis=-1, keepdims=True))
    exp_scores = jnp.exp(scores - row_max)
    probs_low = low(exp_scores / lax.optimization_barrier(jnp.sum(exp_scores, axis=-1, keepdims=True)))
    attended = jnp.einsum('lhqk,lkhd->lqhd', probs_low, value_rows, precision=HIGH)
    attended = low(low_back(attended.reshape(latent_count, seq_length, model_width)))
    attn_out = low_back(project(attended, proj_weight) + proj_bias)
    middle = inputs + gate_one[:, None, :] * attn_out
    second_low = low(modulate(middle, shift_two, scale_two))
    hidden_pre = low_back(project(second_low, fc1_weight) + fc1_bias)
    hidden_low = low(jax.nn.gelu(hidden_pre, approximate=True))
    branch_out = low_back(project(hidden_low, fc2_weight) + fc2_bias)
    return middle + gate_two[:, None, :] * branch_out

def reference(latents_in, conditioning, ada_weight, ada_bias, qkv_weight, qv_bias, proj_weight, proj_bias, fc1_weight, fc1_bias, fc2_weight, fc2_bias, cotangent):
    weights = tuple((array_in.astype(jnp.float32) for array_in in (ada_weight, ada_bias, qkv_weight, qv_bias, proj_weight, proj_bias, fc1_weight, fc1_bias, fc2_weight, fc2_bias)))
    blocks = LATENTS // LAT_DEV
    inputs = latents_in.astype(jnp.float32).reshape(blocks, LAT_DEV, SEQ, D)
    cond_all = conditioning.astype(jnp.float32).reshape(blocks, LAT_DEV, D)
    upstream = cotangent.astype(jnp.float32).reshape(blocks, LAT_DEV, SEQ, D)

    def one_step(totals, block_rows):
        block_in, block_cond, block_cot = block_rows
        output, pullback = jax.vjp(layer, block_in, block_cond, *weights)
        gradients = pullback(block_cot)
        totals = tuple((total + grad_piece for total, grad_piece in zip(totals, gradients[2:])))
        return (totals, (output, gradients[0], gradients[1]))
    start = tuple((jnp.zeros_like(weight_now) for weight_now in weights))
    totals, (outputs, input_grads, cond_grads) = lax.scan(one_step, start, (inputs, cond_all, upstream))
    grad_ada_w, grad_ada_b, grad_qkv_w, grad_qv_b, grad_proj_w, grad_proj_b, grad_fc1_w, grad_fc1_b, grad_fc2_w, grad_fc2_b = totals
    return (outputs.reshape(TOKENS, D).astype(jnp.bfloat16), input_grads.reshape(TOKENS, D), cond_grads.reshape(LATENTS, D), grad_ada_w, grad_ada_b, grad_qkv_w, grad_qv_b, grad_proj_w, grad_proj_b, grad_fc1_w, grad_fc1_b, grad_fc2_w, grad_fc2_b)
```

```python
import jax
import jax.numpy as jnp
from jax import lax
from jax.sharding import PartitionSpec as P

HEAD_DIM = 64


EPSILON = 1e-06


def layer_norm(values):
    center = values - jnp.mean(values, axis=-1, keepdims=True)
    spread = jnp.mean(center * center, axis=-1, keepdims=True)
    return center * lax.rsqrt(spread + EPSILON)


def modulate(values, shift_rows, scale_rows):
    return layer_norm(values) * (1.0 + scale_rows[:, None, :]) + shift_rows[:, None, :]


def gelu_tanh(values):
    return jax.nn.gelu(values, approximate=True)


def project(inputs, weight):
    return jnp.einsum("lsd,de->lse", inputs, weight, preferred_element_type=jnp.float32)


def project_back(gradient, weight):
    return jnp.einsum("lse,de->lsd", gradient, weight, preferred_element_type=jnp.float32)


def weight_grad(inputs, gradient):
    return jnp.einsum("lsd,lse->de", inputs, gradient, preferred_element_type=jnp.float32)


def column_sums(gradient):
    return jnp.sum(gradient, axis=(0, 1), dtype=jnp.float32)


def rep_bits(rep_count):
    return [1 << i for i in range(rep_count.bit_length() - 1)]


def swap_rep(values, bit, rep_count):
    return lax.ppermute(values, "rep", [(i, i ^ bit) for i in range(rep_count)])


def to_shard(values, hop, shard_count):
    return lax.ppermute(values, "shard", [(i, (i + hop) % shard_count) for i in range(shard_count)])


def gather_near(values, shard_count):
    return [values] + [
        to_shard(values, shard_count - hop, shard_count) for hop in range(1, shard_count)
    ]


def in_order(pieces, shard_at):
    count = len(pieces)
    doubled = jnp.stack(pieces + pieces)
    return lax.dynamic_slice_in_dim(doubled, count - shard_at, count, axis=0)


def column_blocks(weight, width):
    return jnp.concatenate(jnp.split(weight, weight.shape[1] // width, axis=1), axis=0)


def unblock(rows, height):
    return jnp.concatenate(jnp.split(rows, rows.shape[0] // height, axis=0), axis=1)


def wide_matrix(blocks, columns):
    count, rows, width = blocks.shape
    groups = columns // width
    return jnp.concatenate(
        [
            blocks[:, i * rows // groups : (i + 1) * rows // groups].reshape(-1, width)
            for i in range(groups)
        ],
        axis=1,
    )


def block_grad(grad, shard_count):
    rows, columns = grad.shape
    pieces = jnp.split(grad, columns // rows, axis=1)
    return jnp.concatenate([piece.reshape(shard_count, -1, rows) for piece in pieces], axis=1)


def gather_shards(rows, shard_count, shard_at, rep_count, rep_at):
    half = rows.shape[0] // 2
    core = rep_at % 2
    mine = lax.dynamic_slice_in_dim(rows, core * half, half, axis=0)
    fetched = jnp.stack(gather_near(mine, shard_count)[1:])
    other = swap_rep(fetched, 1, rep_count)
    low_rows = jnp.where(core == 0, fetched, other)
    high_rows = jnp.where(core == 0, other, fetched)
    joined = jnp.concatenate([low_rows, high_rows], axis=1)
    return in_order([rows] + [joined[i] for i in range(shard_count - 1)], shard_at)


def reduce_rows(partial, shard_count, shard_at, rep_count, rep_at):
    kept = partial
    bits = rep_bits(rep_count)
    for at, bit in enumerate(bits):
        side = (rep_at >> at) & 1
        half = kept.shape[1] // 2
        sent = lax.dynamic_slice_in_dim(kept, (1 - side) * half, half, axis=1)
        came = swap_rep(sent.astype(jnp.bfloat16), bit, rep_count)
        kept = lax.dynamic_slice_in_dim(kept, side * half, half, axis=1) + came.astype(jnp.float32)
    total = lax.dynamic_index_in_dim(kept, shard_at, 0, keepdims=False)
    for hop in range(1, shard_count):
        target = (shard_at + hop) % shard_count
        sent = lax.dynamic_index_in_dim(kept, target, 0, keepdims=False)
        came = to_shard(sent.astype(jnp.bfloat16), hop, shard_count)
        total = total + came.astype(jnp.float32)
    whole = total.astype(jnp.bfloat16)
    for at in range(len(bits) - 1, -1, -1):
        side = (rep_at >> at) & 1
        other = swap_rep(whole, bits[at], rep_count)
        whole = jnp.concatenate(
            [jnp.where(side == 0, whole, other), jnp.where(side == 0, other, whole)], axis=0
        )
    return whole.astype(jnp.float32)


def sum_small(partial, shard_count, shard_at, rep_count):
    for bit in rep_bits(rep_count):
        partial = partial + swap_rep(partial, bit, rep_count)
    total = lax.dynamic_index_in_dim(partial, shard_at, 0, keepdims=False)
    for hop in range(1, shard_count):
        target = (shard_at + hop) % shard_count
        sent = lax.dynamic_index_in_dim(partial, target, 0, keepdims=False)
        total = total + to_shard(sent, hop, shard_count)
    return total


def shards(
    latents_in,
    conditioning,
    ada_weight,
    ada_bias,
    qkv_weight,
    qv_bias,
    proj_weight,
    proj_bias,
    fc1_weight,
    fc1_bias,
    fc2_weight,
    fc2_bias,
    cotangent,
):
    latent_count = conditioning.shape[0]
    model_width = conditioning.shape[1]
    seq_length = latents_in.shape[0] // latent_count
    head_count = model_width // HEAD_DIM
    softmax_scale = HEAD_DIM ** (-0.5)
    shard_count = lax.axis_size("shard")
    rep_count = lax.axis_size("rep")
    shard_at = lax.axis_index("shard")
    rep_at = lax.axis_index("rep")
    part = model_width // shard_count
    small_rows = jnp.concatenate([qv_bias, proj_bias, fc1_bias, fc2_bias])
    small_rows = small_rows.reshape(-1, model_width)
    first_pack = gather_near(jnp.concatenate([conditioning, small_rows], axis=0), shard_count)
    cond_near = jnp.concatenate([piece[:latent_count] for piece in first_pack], axis=0)
    qkv_blocks = gather_shards(column_blocks(qkv_weight, model_width), shard_count, shard_at, rep_count, rep_at)
    late_blocks = gather_shards(
        jnp.concatenate([proj_weight, column_blocks(fc1_weight, model_width), fc2_weight], axis=0),
        shard_count, shard_at, rep_count, rep_at,
    )
    silu_near = jax.nn.silu(cond_near.astype(jnp.float32)).astype(jnp.bfloat16)
    silu_mine = lax.dynamic_slice_in_dim(silu_near, shard_at * part, part, axis=1)
    mod_part = jnp.dot(silu_mine, ada_weight, preferred_element_type=jnp.float32)
    wide_bias = lax.dynamic_update_slice_in_dim(
        jnp.zeros((ada_weight.shape[1],), jnp.float32), ada_bias.astype(jnp.float32),
        shard_at * ada_bias.shape[0], axis=0,
    )
    mod_part = (mod_part + wide_bias).reshape(shard_count, latent_count, -1)
    modulation = mod_part[0]
    for hop in range(1, shard_count):
        modulation = modulation + to_shard(mod_part[hop], hop, shard_count)
    small_all = in_order([piece[latent_count:] for piece in first_pack], shard_at)
    small_all = small_all.reshape(shard_count, -1)
    edges = [0]
    for vector in (qv_bias, proj_bias, fc1_bias, fc2_bias):
        edges.append(edges[-1] + vector.shape[0])
    qv_offsets, proj_offsets, up_offsets, down_offsets = (
        small_all[:, edges[i] : edges[i + 1]].reshape(-1) for i in range(4)
    )
    qkv_matrix = wide_matrix(qkv_blocks, qkv_weight.shape[1])
    proj_matrix = late_blocks[:, :part].reshape(model_width, model_width)
    up_rows = part * (fc1_weight.shape[1] // model_width)
    up_matrix = wide_matrix(late_blocks[:, part : part + up_rows], fc1_weight.shape[1])
    down_matrix = late_blocks[:, part + up_rows :].reshape(-1, model_width)
    inputs = latents_in.astype(jnp.float32).reshape(latent_count, seq_length, model_width)
    _, silu_pull = jax.vjp(jax.nn.silu, conditioning.astype(jnp.float32))
    shift_one, scale_one, gate_one, shift_two, scale_two, gate_two = jnp.split(
        modulation, 6, axis=1
    )
    first_in, first_pull = jax.vjp(modulate, inputs, shift_one, scale_one)
    first_low = first_in.astype(jnp.bfloat16)
    zero_bias = jnp.zeros((model_width,), jnp.bfloat16)
    full_bias = jnp.concatenate(
        [qv_offsets[:model_width], zero_bias, qv_offsets[model_width:]]
    ).astype(jnp.float32)
    qkv_low = (project(first_low, qkv_matrix) + full_bias).astype(jnp.bfloat16)
    qkv_low = qkv_low.reshape(latent_count, seq_length, 3, head_count, HEAD_DIM)
    queries = qkv_low[:, :, 0]
    key_rows = qkv_low[:, :, 1]
    value_rows = qkv_low[:, :, 2]
    scores = (
        jnp.einsum("lqhd,lkhd->lhqk", queries, key_rows, preferred_element_type=jnp.float32)
        * softmax_scale
    )
    row_max = jnp.max(scores, axis=-1, keepdims=True)
    log_total = row_max + jnp.log(jnp.sum(jnp.exp(scores - row_max), axis=-1, keepdims=True))
    probs_fwd = jnp.exp(scores - log_total).astype(jnp.bfloat16)
    attended = jnp.einsum(
        "lhqk,lkhd->lqhd", probs_fwd, value_rows, preferred_element_type=jnp.float32
    )
    attended_low = attended.reshape(latent_count, seq_length, model_width).astype(jnp.bfloat16)
    attn_out = project(attended_low, proj_matrix) + proj_offsets.astype(jnp.float32)
    middle = inputs + gate_one[:, None, :] * attn_out
    second_in, second_pull = jax.vjp(modulate, middle, shift_two, scale_two)
    second_low = second_in.astype(jnp.bfloat16)
    hidden_pre = project(second_low, up_matrix) + up_offsets.astype(jnp.float32)
    hidden_act, gelu_pull = jax.vjp(gelu_tanh, hidden_pre)
    hidden_low = hidden_act.astype(jnp.bfloat16)
    branch_out = project(hidden_low, down_matrix) + down_offsets.astype(jnp.float32)
    result = middle + gate_two[:, None, :] * branch_out
    upstream = cotangent.astype(jnp.float32).reshape(latent_count, seq_length, model_width)
    down_grad = (gate_two[:, None, :] * upstream).astype(jnp.bfloat16)
    gate_two_grad = jnp.sum(upstream * branch_out, axis=1)
    down_w_grad = weight_grad(hidden_low, down_grad)
    down_b_grad = column_sums(down_grad)
    hidden_grad = gelu_pull(project_back(down_grad, down_matrix))[0].astype(jnp.bfloat16)
    up_w_grad = weight_grad(second_low, hidden_grad)
    up_b_grad = column_sums(hidden_grad)
    early = jnp.concatenate(
        [
            down_w_grad.reshape(shard_count, -1, model_width),
            block_grad(up_w_grad, shard_count),
        ],
        axis=1,
    )
    early_sum = reduce_rows(early, shard_count, shard_at, rep_count, rep_at)
    middle_part, shift_two_grad, scale_two_grad = second_pull(project_back(hidden_grad, up_matrix))
    middle_grad = upstream + middle_part
    attn_grad = (gate_one[:, None, :] * middle_grad).astype(jnp.bfloat16)
    gate_one_grad = jnp.sum(middle_grad * attn_out, axis=1)
    proj_w_grad = weight_grad(attended_low, attn_grad)
    proj_b_grad = column_sums(attn_grad)
    attended_grad = project_back(attn_grad, proj_matrix).astype(jnp.bfloat16)
    attended_grad = attended_grad.reshape(latent_count, seq_length, head_count, HEAD_DIM)
    scores_again = (
        jnp.einsum("lqhd,lkhd->lhqk", queries, key_rows, preferred_element_type=jnp.float32)
        * softmax_scale
    )
    probs_again = jnp.exp(scores_again - log_total)
    value_grad = jnp.einsum(
        "lhqk,lqhd->lkhd",
        probs_again.astype(jnp.bfloat16),
        attended_grad,
        preferred_element_type=jnp.float32,
    )
    probs_grad = jnp.einsum(
        "lqhd,lkhd->lhqk", attended_grad, value_rows, preferred_element_type=jnp.float32
    )
    score_grad = probs_again * (
        probs_grad - jnp.sum(probs_again * probs_grad, axis=-1, keepdims=True)
    )
    score_low = score_grad.astype(jnp.bfloat16)
    query_grad = (
        jnp.einsum("lhqk,lkhd->lqhd", score_low, key_rows, preferred_element_type=jnp.float32)
        * softmax_scale
    )
    key_grad = (
        jnp.einsum("lhqk,lqhd->lkhd", score_low, queries, preferred_element_type=jnp.float32)
        * softmax_scale
    )
    qkv_grad = jnp.stack([query_grad, key_grad, value_grad], axis=2)
    qkv_grad = qkv_grad.reshape(latent_count, seq_length, 3 * model_width).astype(jnp.bfloat16)
    qkv_w_grad = weight_grad(first_low, qkv_grad)
    qkv_sums = column_sums(qkv_grad)
    qv_b_grad = jnp.concatenate([qkv_sums[:model_width], qkv_sums[2 * model_width :]])
    input_part, shift_one_grad, scale_one_grad = first_pull(project_back(qkv_grad, qkv_matrix))
    input_grad = middle_grad + input_part
    mod_grad = jnp.concatenate(
        [
            shift_one_grad,
            scale_one_grad,
            gate_one_grad,
            shift_two_grad,
            scale_two_grad,
            gate_two_grad,
        ],
        axis=1,
    ).astype(jnp.bfloat16)
    late = jnp.concatenate(
        [proj_w_grad.reshape(shard_count, -1, model_width), block_grad(qkv_w_grad, shard_count)],
        axis=1,
    )
    late_sum = reduce_rows(late, shard_count, shard_at, rep_count, rep_at)
    small_grads = jnp.concatenate(
        [
            vector.reshape(shard_count, -1)
            for vector in (qv_b_grad, proj_b_grad, up_b_grad, down_b_grad)
        ],
        axis=1,
    )
    small_final = sum_small(small_grads, shard_count, shard_at, rep_count)
    mod_near = jnp.concatenate(gather_near(mod_grad, shard_count), axis=0)
    cond_part = jnp.einsum("le,de->ld", mod_near, ada_weight, preferred_element_type=jnp.float32)
    cond_part = cond_part.reshape(shard_count, latent_count, part)
    pieces = [cond_part[0]]
    for hop in range(1, shard_count):
        pieces.append(to_shard(cond_part[hop], hop, shard_count))
    pieces = pieces[:1] + pieces[:0:-1]
    cond_grad = in_order(pieces, shard_at)
    cond_grad = cond_grad.transpose(1, 0, 2).reshape(latent_count, model_width)
    cond_grad = silu_pull(cond_grad)[0]
    mod_all, silu_all = mod_near, silu_mine
    for bit in rep_bits(rep_count)[::-1]:
        mod_all = jnp.concatenate([mod_all, swap_rep(mod_all, bit, rep_count)], axis=0)
        silu_all = jnp.concatenate([silu_all, swap_rep(silu_all, bit, rep_count)], axis=0)
    final_ada_w = jnp.einsum("ld,le->de", silu_all, mod_all, preferred_element_type=jnp.float32)
    bias_cols = ada_bias.shape[0]
    final_ada_b = jnp.sum(
        lax.dynamic_slice_in_dim(mod_all, shard_at * bias_cols, bias_cols, axis=1),
        axis=0,
        dtype=jnp.float32,
    )
    down_rows = fc2_weight.shape[0]
    final_down_w = early_sum[:down_rows]
    final_up_w = unblock(early_sum[down_rows:], part)
    final_proj_w = late_sum[:part]
    final_qkv_w = unblock(late_sum[part:], part)
    final_qv_b, final_proj_b, final_up_b, final_down_b = (
        small_final[edges[i] : edges[i + 1]] for i in range(4)
    )
    return (
        result.reshape(latent_count * seq_length, model_width).astype(jnp.bfloat16),
        input_grad.reshape(latent_count * seq_length, model_width),
        cond_grad,
        final_ada_w,
        final_ada_b,
        final_qkv_w,
        final_qv_b,
        final_proj_w,
        final_proj_b,
        final_up_w,
        final_up_b,
        final_down_w,
        final_down_b,
    )


def solution(mesh):
    return jax.shard_map(
        shards,
        mesh=mesh,
        in_specs=(
            P(("shard", "rep"), None),
            P(("shard", "rep"), None),
            P("shard", None),
            P("shard"),
            P("shard", None),
            P("shard"),
            P("shard", None),
            P("shard"),
            P("shard", None),
            P("shard"),
            P("shard", None),
            P("shard"),
            P(("shard", "rep"), None),
        ),
        out_specs=(
            P(("shard", "rep"), None),
            P(("shard", "rep"), None),
            P(("shard", "rep"), None),
            P("shard", None),
            P("shard"),
            P("shard", None),
            P("shard"),
            P("shard", None),
            P("shard"),
            P("shard", None),
            P("shard"),
            P("shard", None),
            P("shard"),
        ),
        check_vma=False,
    )
```

```python
import functools

import jax
import jax.numpy as jnp
from jax import lax
from jax.experimental import pallas as pl
from jax.experimental.pallas import tpu as pltpu
from jax.sharding import PartitionSpec as P

HEAD_DIM = 64


EPSILON = 1e-06


def layer_norm(values):
    center = values - jnp.mean(values, axis=-1, keepdims=True)
    spread = jnp.mean(center * center, axis=-1, keepdims=True)
    return center * lax.rsqrt(spread + EPSILON)


def modulate(values, shift_rows, scale_rows):
    return layer_norm(values) * (1.0 + scale_rows[:, None, :]) + shift_rows[:, None, :]


def gelu_tanh(values):
    return jax.nn.gelu(values, approximate=True)


def project(inputs, weight):
    return jnp.einsum("lsd,de->lse", inputs, weight, preferred_element_type=jnp.float32)


def project_back(gradient, weight):
    return jnp.einsum("lse,de->lsd", gradient, weight, preferred_element_type=jnp.float32)


def weight_grad(inputs, gradient):
    return jnp.einsum("lsd,lse->de", inputs, gradient, preferred_element_type=jnp.float32)


def column_sums(gradient):
    return jnp.sum(gradient, axis=(0, 1), dtype=jnp.float32)


def rep_bits(rep_count):
    return [1 << i for i in range(rep_count.bit_length() - 1)]


def swap_rep(values, bit, rep_count):
    return lax.ppermute(values, "rep", [(i, i ^ bit) for i in range(rep_count)])


def to_shard(values, hop, shard_count):
    return lax.ppermute(values, "shard", [(i, (i + hop) % shard_count) for i in range(shard_count)])


def gather_near(values, shard_count):
    return [values] + [
        to_shard(values, shard_count - hop, shard_count) for hop in range(1, shard_count)
    ]


def in_order(pieces, shard_at):
    count = len(pieces)
    doubled = jnp.stack(pieces + pieces)
    return lax.dynamic_slice_in_dim(doubled, count - shard_at, count, axis=0)


def column_blocks(weight, width):
    return jnp.concatenate(jnp.split(weight, weight.shape[1] // width, axis=1), axis=0)


def unblock(rows, height):
    return jnp.concatenate(jnp.split(rows, rows.shape[0] // height, axis=0), axis=1)


def wide_matrix(blocks, columns):
    count, rows, width = blocks.shape
    groups = columns // width
    return jnp.concatenate(
        [
            blocks[:, i * rows // groups : (i + 1) * rows // groups].reshape(-1, width)
            for i in range(groups)
        ],
        axis=1,
    )


def block_grad(grad, shard_count):
    rows, columns = grad.shape
    pieces = jnp.split(grad, columns // rows, axis=1)
    return jnp.concatenate([piece.reshape(shard_count, -1, rows) for piece in pieces], axis=1)


def gather_shards(rows, shard_count, shard_at, rep_count, rep_at):
    half = rows.shape[0] // 2
    core = rep_at % 2
    mine = lax.dynamic_slice_in_dim(rows, core * half, half, axis=0)
    fetched = jnp.stack(gather_near(mine, shard_count)[1:])
    other = swap_rep(fetched, 1, rep_count)
    low_rows = jnp.where(core == 0, fetched, other)
    high_rows = jnp.where(core == 0, other, fetched)
    joined = jnp.concatenate([low_rows, high_rows], axis=1)
    return in_order([rows] + [joined[i] for i in range(shard_count - 1)], shard_at)


def reduce_kernel(
    shard_count, rep_count, plans, half_mod, lane_total, *refs
):
    refs = list(refs)
    lane_refs = [refs.pop(0) for _ in range(lane_total)]
    small_ref, mod_ref, ada_ref = refs.pop(0), refs.pop(0), refs.pop(0)
    lane_outs = [refs.pop(0) for _ in range(lane_total)]
    small_out, mod_out, cond_out = refs.pop(0), refs.pop(0), refs.pop(0)
    bits_total = rep_count.bit_length() - 1
    lane_bufs = []
    for _ in range(lane_total):
        stages = [[refs.pop(0) for _ in range(3)] for _ in range(bits_total)]
        lane_bufs.append((stages, refs.pop(0), refs.pop(0), refs.pop(0)))
    small_acc, small_came, small_z = refs.pop(0), refs.pop(0), refs.pop(0)
    mod_buf, cond_send, cond_came = refs.pop(0), refs.pop(0), refs.pop(0)
    send_sems, recv_sems = refs
    shard_at, rep_at = lax.axis_index("shard"), lax.axis_index("rep")
    bits = [1 << i for i in range(bits_total)]
    sides = [lax.rem(rep_at // bit, 2) for bit in bits]
    peers = [rep_at + bit - 2 * bit * side for bit, side in zip(bits, sides)]
    targets = [lax.rem(shard_at + hop, shard_count) for hop in range(shard_count)]

    barrier = pltpu.get_barrier_semaphore()
    partners = [{"rep": peer} for peer in peers] + [{"shard": at} for at in targets[1:]]
    for partner in partners:
        pl.semaphore_signal(
            barrier, inc=1, device_id=partner, device_id_type=pl.DeviceIdType.MESH
        )
    pl.semaphore_wait(barrier, len(partners))
    used = [0]

    def send(source, landing, partner):
        at = used[0]
        used[0] += 1
        copy = pltpu.make_async_remote_copy(
            src_ref=source,
            dst_ref=landing,
            send_sem=send_sems.at[at],
            recv_sem=recv_sems.at[at],
            device_id=partner,
            device_id_type=pl.DeviceIdType.MESH,
        )
        copy.start()
        return copy

    def lane_steps(lane):
        (order, halved), source = plans[lane], lane_refs[lane]
        stages, z_send, z_came, final = lane_bufs[lane]
        offset = 0
        for at, split, (sent, came, kept) in zip(order, halved, stages):
            rows = sent.shape[1]
            side = sides[at]
            if split:
                away = pl.multiple_of((1 - side) * rows, 16)
                stay = pl.multiple_of(side * rows, 16)
                sent[...] = source[:, pl.ds(away, rows), :].astype(jnp.bfloat16)
            else:
                sent[...] = source[...].astype(jnp.bfloat16)
            copy = send(sent, came, {"rep": peers[at]})
            yield
            copy.wait()
            if split:
                kept[...] = source[:, pl.ds(stay, rows), :] + came[...].astype(jnp.float32)
                offset = offset + side * rows
            else:
                kept[...] = sent[...].astype(jnp.float32) + came[...].astype(jnp.float32)
            source = kept
        z_send[...] = source[...].astype(jnp.bfloat16)
        copies = [
            send(z_send.at[targets[hop]], z_came.at[hop - 1], {"shard": targets[hop]})
            for hop in range(1, shard_count)
        ]
        yield
        total = source[shard_at]
        for copy in copies:
            copy.wait()
        for hop in range(1, shard_count):
            total = total + z_came[hop - 1].astype(jnp.float32)
        rows = total.shape[0]
        final[pl.ds(pl.multiple_of(offset, 16), rows), :] = total.astype(jnp.bfloat16)
        for at, split in list(zip(order, halved))[::-1]:
            if not split:
                continue
            place = final.at[pl.ds(pl.multiple_of(offset, 16), rows), :]
            copy = send(place, place, {"rep": peers[at]})
            yield
            copy.wait()
            offset = offset - sides[at] * rows
            rows = rows * 2
        lane_outs[lane][...] = final[...].astype(jnp.float32)

    def small_steps():
        small_acc[0] = small_ref[...]
        for at in range(bits_total):
            copy = send(small_acc.at[at], small_came.at[at], {"rep": peers[at]})
            yield
            copy.wait()
            small_acc[at + 1] = small_acc[at] + small_came[at]
        copies = [
            send(
                small_acc.at[bits_total, targets[hop]],
                small_z.at[hop - 1],
                {"shard": targets[hop]},
            )
            for hop in range(1, shard_count)
        ]
        yield
        total = small_acc[bits_total, shard_at]
        for copy in copies:
            copy.wait()
        for hop in range(1, shard_count):
            total = total + small_z[hop - 1]
        small_out[...] = total

    def mod_steps():
        mod_buf[0] = mod_ref[...]
        copies = [
            send(mod_buf.at[0], mod_buf.at[shard_count - hop], {"shard": targets[hop]})
            for hop in range(1, shard_count)
        ]
        yield
        for copy in copies:
            copy.wait()
        filled = shard_count
        copy = None
        cond_copies = []
        for at in range(bits_total)[::-1]:
            copy = send(
                mod_buf.at[pl.ds(0, filled)], mod_buf.at[pl.ds(filled, filled)], {"rep": peers[at]}
            )
            if filled == shard_count:
                for near in range(shard_count):
                    rows = mod_buf[near][:, :half_mod]
                    dims = (((1,), (1,)), ((), ()))
                    first = lax.dot_general(
                        rows, ada_ref[:, :half_mod], dims, preferred_element_type=jnp.float32
                    )
                    second = lax.dot_general(
                        rows, ada_ref[:, half_mod:], dims, preferred_element_type=jnp.float32
                    )
                    lat = rows.shape[0] // 2
                    cond_send[near] = first[:lat] + second[lat:]
                cond_copies = [
                    send(cond_send.at[hop], cond_came.at[hop - 1], {"shard": targets[hop]})
                    for hop in range(1, shard_count)
                ]
            yield
            copy.wait()
            filled = filled * 2
        for done in cond_copies:
            done.wait()
        cond_out[0] = cond_send[0]
        for hop in range(1, shard_count):
            cond_out[hop] = cond_came[hop - 1]
        mod_out[...] = mod_buf[...]

    running = [lane_steps(lane) for lane in range(lane_total)] + [mod_steps(), small_steps()]
    while running:
        running = [steps for steps in running if next(steps, "end") is None]


def reduce_all(lanes, small, mod_slot, ada_padded, shard_count, rep_count, half_mod):
    bits_total = rep_count.bit_length() - 1
    plans, scratch, outs = [], [], []
    copies = 0
    for at, lane in enumerate(lanes):
        count, rows, width = lane.shape
        order = list(range(bits_total))
        if at % 2 == 1:
            order = order[:1] + order[:0:-1]
        halved = []
        for _ in order:
            split = rows % 32 == 0
            halved.append(split)
            rows = rows // 2 if split else rows
            scratch.append(pltpu.VMEM((count, rows, width), jnp.bfloat16))
            scratch.append(pltpu.VMEM((count, rows, width), jnp.bfloat16))
            scratch.append(pltpu.VMEM((count, rows, width), jnp.float32))
        scratch.append(pltpu.VMEM((count, rows, width), jnp.bfloat16))
        scratch.append(pltpu.VMEM((count - 1, rows, width), jnp.bfloat16))
        scratch.append(pltpu.VMEM((lane.shape[1], width), jnp.bfloat16))
        plans.append((order, halved))
        outs.append(jax.ShapeDtypeStruct((lane.shape[1], width), jnp.float32))
        copies += 2 * bits_total + shard_count
    slots = shard_count * rep_count
    lat = mod_slot.shape[0] // 2
    scratch += [
        pltpu.VMEM((bits_total + 1,) + small.shape, jnp.float32),
        pltpu.VMEM((bits_total,) + small.shape, jnp.float32),
        pltpu.VMEM((shard_count - 1,) + small.shape[1:], jnp.float32),
        pltpu.VMEM((slots,) + mod_slot.shape, jnp.bfloat16),
        pltpu.VMEM((shard_count, lat, 128), jnp.float32),
        pltpu.VMEM((shard_count - 1, lat, 128), jnp.float32),
    ]
    copies += 2 * bits_total + 3 * shard_count
    scratch += [pltpu.SemaphoreType.DMA((copies,)), pltpu.SemaphoreType.DMA((copies,))]
    outs += [
        jax.ShapeDtypeStruct(small.shape[1:], jnp.float32),
        jax.ShapeDtypeStruct((slots,) + mod_slot.shape, jnp.bfloat16),
        jax.ShapeDtypeStruct((shard_count, lat, 128), jnp.float32),
    ]
    return pl.pallas_call(
        functools.partial(reduce_kernel, shard_count, rep_count, plans, half_mod, len(lanes)),
        out_shape=outs,
        in_specs=[pl.BlockSpec(memory_space=pltpu.VMEM)] * (len(lanes) + 3),
        out_specs=[pl.BlockSpec(memory_space=pltpu.VMEM)] * len(outs),
        scratch_shapes=scratch,
        compiler_params=pltpu.CompilerParams(
            collective_id=0, has_side_effects=True, vmem_limit_bytes=56 * 1024 * 1024
        ),
    )(*lanes, small, mod_slot, ada_padded)


def shards(
    latents_in,
    conditioning,
    ada_weight,
    ada_bias,
    qkv_weight,
    qv_bias,
    proj_weight,
    proj_bias,
    fc1_weight,
    fc1_bias,
    fc2_weight,
    fc2_bias,
    cotangent,
):
    latent_count = conditioning.shape[0]
    model_width = conditioning.shape[1]
    seq_length = latents_in.shape[0] // latent_count
    head_count = model_width // HEAD_DIM
    softmax_scale = HEAD_DIM ** (-0.5)
    shard_count = lax.axis_size("shard")
    rep_count = lax.axis_size("rep")
    shard_at = lax.axis_index("shard")
    rep_at = lax.axis_index("rep")
    part = model_width // shard_count
    small_rows = jnp.concatenate([qv_bias, proj_bias, fc1_bias, fc2_bias])
    small_rows = small_rows.reshape(-1, model_width)
    first_pack = gather_near(jnp.concatenate([conditioning, small_rows], axis=0), shard_count)
    cond_near = jnp.concatenate([piece[:latent_count] for piece in first_pack], axis=0)
    qkv_blocks = gather_shards(column_blocks(qkv_weight, model_width), shard_count, shard_at, rep_count, rep_at)
    late_blocks = gather_shards(
        jnp.concatenate([proj_weight, column_blocks(fc1_weight, model_width), fc2_weight], axis=0),
        shard_count, shard_at, rep_count, rep_at,
    )
    silu_near = jax.nn.silu(cond_near.astype(jnp.float32)).astype(jnp.bfloat16)
    silu_mine = lax.dynamic_slice_in_dim(silu_near, shard_at * part, part, axis=1)
    mod_part = jnp.dot(silu_mine, ada_weight, preferred_element_type=jnp.float32)
    wide_bias = lax.dynamic_update_slice_in_dim(
        jnp.zeros((ada_weight.shape[1],), jnp.float32), ada_bias.astype(jnp.float32),
        shard_at * ada_bias.shape[0], axis=0,
    )
    mod_part = (mod_part + wide_bias).reshape(shard_count, latent_count, -1)
    modulation = mod_part[0]
    for hop in range(1, shard_count):
        modulation = modulation + to_shard(mod_part[hop], hop, shard_count)
    small_all = in_order([piece[latent_count:] for piece in first_pack], shard_at)
    small_all = small_all.reshape(shard_count, -1)
    edges = [0]
    for vector in (qv_bias, proj_bias, fc1_bias, fc2_bias):
        edges.append(edges[-1] + vector.shape[0])
    qv_offsets, proj_offsets, up_offsets, down_offsets = (
        small_all[:, edges[i] : edges[i + 1]].reshape(-1) for i in range(4)
    )
    qkv_matrix = wide_matrix(qkv_blocks, qkv_weight.shape[1])
    proj_matrix = late_blocks[:, :part].reshape(model_width, model_width)
    up_rows = part * (fc1_weight.shape[1] // model_width)
    up_matrix = wide_matrix(late_blocks[:, part : part + up_rows], fc1_weight.shape[1])
    down_matrix = late_blocks[:, part + up_rows :].reshape(-1, model_width)
    inputs = latents_in.astype(jnp.float32).reshape(latent_count, seq_length, model_width)
    _, silu_pull = jax.vjp(jax.nn.silu, conditioning.astype(jnp.float32))
    shift_one, scale_one, gate_one, shift_two, scale_two, gate_two = jnp.split(
        modulation, 6, axis=1
    )
    first_in, first_pull = jax.vjp(modulate, inputs, shift_one, scale_one)
    first_low = first_in.astype(jnp.bfloat16)
    zero_bias = jnp.zeros((model_width,), jnp.bfloat16)
    full_bias = jnp.concatenate(
        [qv_offsets[:model_width], zero_bias, qv_offsets[model_width:]]
    ).astype(jnp.float32)
    qkv_low = (project(first_low, qkv_matrix) + full_bias).astype(jnp.bfloat16)
    qkv_low = qkv_low.reshape(latent_count, seq_length, 3, head_count, HEAD_DIM)
    queries = qkv_low[:, :, 0]
    key_rows = qkv_low[:, :, 1]
    value_rows = qkv_low[:, :, 2]
    scores = (
        jnp.einsum("lqhd,lkhd->lhqk", queries, key_rows, preferred_element_type=jnp.float32)
        * softmax_scale
    )
    row_max = jnp.max(scores, axis=-1, keepdims=True)
    log_total = row_max + jnp.log(jnp.sum(jnp.exp(scores - row_max), axis=-1, keepdims=True))
    probs_fwd = jnp.exp(scores - log_total).astype(jnp.bfloat16)
    attended = jnp.einsum(
        "lhqk,lkhd->lqhd", probs_fwd, value_rows, preferred_element_type=jnp.float32
    )
    attended_low = attended.reshape(latent_count, seq_length, model_width).astype(jnp.bfloat16)
    attn_out = project(attended_low, proj_matrix) + proj_offsets.astype(jnp.float32)
    middle = inputs + gate_one[:, None, :] * attn_out
    second_in, second_pull = jax.vjp(modulate, middle, shift_two, scale_two)
    second_low = second_in.astype(jnp.bfloat16)
    hidden_pre = project(second_low, up_matrix) + up_offsets.astype(jnp.float32)
    hidden_act, gelu_pull = jax.vjp(gelu_tanh, hidden_pre)
    hidden_low = hidden_act.astype(jnp.bfloat16)
    branch_out = project(hidden_low, down_matrix) + down_offsets.astype(jnp.float32)
    result = middle + gate_two[:, None, :] * branch_out
    upstream = cotangent.astype(jnp.float32).reshape(latent_count, seq_length, model_width)
    down_grad = (gate_two[:, None, :] * upstream).astype(jnp.bfloat16)
    gate_two_grad = jnp.sum(upstream * branch_out, axis=1)
    down_w_grad = weight_grad(hidden_low, down_grad)
    down_b_grad = column_sums(down_grad)
    hidden_grad = gelu_pull(project_back(down_grad, down_matrix))[0].astype(jnp.bfloat16)
    up_w_grad = weight_grad(second_low, hidden_grad)
    up_b_grad = column_sums(hidden_grad)
    middle_part, shift_two_grad, scale_two_grad = second_pull(project_back(hidden_grad, up_matrix))
    middle_grad = upstream + middle_part
    attn_grad = (gate_one[:, None, :] * middle_grad).astype(jnp.bfloat16)
    gate_one_grad = jnp.sum(middle_grad * attn_out, axis=1)
    proj_w_grad = weight_grad(attended_low, attn_grad)
    proj_b_grad = column_sums(attn_grad)
    attended_grad = project_back(attn_grad, proj_matrix).astype(jnp.bfloat16)
    attended_grad = attended_grad.reshape(latent_count, seq_length, head_count, HEAD_DIM)
    scores_again = (
        jnp.einsum("lqhd,lkhd->lhqk", queries, key_rows, preferred_element_type=jnp.float32)
        * softmax_scale
    )
    probs_again = jnp.exp(scores_again - log_total)
    value_grad = jnp.einsum(
        "lhqk,lqhd->lkhd",
        probs_again.astype(jnp.bfloat16),
        attended_grad,
        preferred_element_type=jnp.float32,
    )
    probs_grad = jnp.einsum(
        "lqhd,lkhd->lhqk", attended_grad, value_rows, preferred_element_type=jnp.float32
    )
    score_grad = probs_again * (
        probs_grad - jnp.sum(probs_again * probs_grad, axis=-1, keepdims=True)
    )
    score_low = score_grad.astype(jnp.bfloat16)
    query_grad = (
        jnp.einsum("lhqk,lkhd->lqhd", score_low, key_rows, preferred_element_type=jnp.float32)
        * softmax_scale
    )
    key_grad = (
        jnp.einsum("lhqk,lqhd->lkhd", score_low, queries, preferred_element_type=jnp.float32)
        * softmax_scale
    )
    qkv_grad = jnp.stack([query_grad, key_grad, value_grad], axis=2)
    qkv_grad = qkv_grad.reshape(latent_count, seq_length, 3 * model_width).astype(jnp.bfloat16)
    qkv_w_grad = weight_grad(first_low, qkv_grad)
    qkv_sums = column_sums(qkv_grad)
    qv_b_grad = jnp.concatenate([qkv_sums[:model_width], qkv_sums[2 * model_width :]])
    input_part, shift_one_grad, scale_one_grad = first_pull(project_back(qkv_grad, qkv_matrix))
    input_grad = middle_grad + input_part
    mod_grad = jnp.concatenate(
        [
            shift_one_grad,
            scale_one_grad,
            gate_one_grad,
            shift_two_grad,
            scale_two_grad,
            gate_two_grad,
        ],
        axis=1,
    ).astype(jnp.bfloat16)
    late = jnp.concatenate(
        [proj_w_grad.reshape(shard_count, -1, model_width), block_grad(qkv_w_grad, shard_count)],
        axis=1,
    )
    lanes = (
        down_w_grad.reshape(shard_count, -1, model_width),
        block_grad(up_w_grad, shard_count),
        late,
    )
    small_grads = jnp.concatenate(
        [
            vector.reshape(shard_count, -1)
            for vector in (qv_b_grad, proj_b_grad, up_b_grad, down_b_grad)
        ],
        axis=1,
    )
    small_width = small_grads.shape[1]
    small_grads = jnp.pad(small_grads, ((0, 0), (0, 1024 - small_width)))
    half_mod, half_silu = mod_grad.shape[1] // 2, model_width // 2
    silu_mid = jax.nn.silu(conditioning.astype(jnp.float32)).astype(jnp.bfloat16)
    silu_fold = jnp.concatenate([silu_mid[:, :half_silu], silu_mid[:, half_silu:]], axis=0)
    mod_slot = jnp.concatenate(
        [
            jnp.concatenate([mod_grad[:, :half_mod], mod_grad[:, half_mod:]], axis=0),
            jnp.pad(silu_fold, ((0, 0), (0, 256 - half_silu))),
        ],
        axis=1,
    )
    down_sum, up_sum, late_sum, small_final, mod_slots, cond_near_grad = reduce_all(
        lanes,
        small_grads.reshape(shard_count, 8, 128),
        mod_slot,
        jnp.pad(ada_weight, ((0, 128 - part), (0, 0))),
        shard_count,
        rep_count,
        half_mod,
    )
    small_final = small_final.reshape(-1)
    pieces = [cond_near_grad[i, :, :part] for i in range(shard_count)]
    cond_grad = in_order(pieces[:1] + pieces[:0:-1], shard_at)
    cond_grad = cond_grad.transpose(1, 0, 2).reshape(latent_count, model_width)
    cond_grad = silu_pull(cond_grad)[0]
    top, bottom = mod_slots[:, :latent_count], mod_slots[:, latent_count:]
    mod_all = jnp.concatenate([top[:, :, :half_mod], bottom[:, :, :half_mod]], axis=2)
    mod_all = mod_all.reshape(-1, 2 * half_mod)
    silu_all = jnp.concatenate(
        [
            top[:, :, half_mod : half_mod + half_silu],
            bottom[:, :, half_mod : half_mod + half_silu],
        ],
        axis=2,
    ).reshape(-1, model_width)
    silu_all = lax.dynamic_slice_in_dim(silu_all, shard_at * part, part, axis=1)
    final_ada_w = jnp.einsum("ld,le->de", silu_all, mod_all, preferred_element_type=jnp.float32)
    bias_cols = ada_bias.shape[0]
    final_ada_b = jnp.sum(
        lax.dynamic_slice_in_dim(mod_all, shard_at * bias_cols, bias_cols, axis=1),
        axis=0,
        dtype=jnp.float32,
    )
    final_down_w = down_sum
    final_up_w = unblock(up_sum, part)
    final_proj_w = late_sum[:part]
    final_qkv_w = unblock(late_sum[part:], part)
    final_qv_b, final_proj_b, final_up_b, final_down_b = (
        small_final[edges[i] : edges[i + 1]] for i in range(4)
    )
    return (
        result.reshape(latent_count * seq_length, model_width).astype(jnp.bfloat16),
        input_grad.reshape(latent_count * seq_length, model_width),
        cond_grad,
        final_ada_w,
        final_ada_b,
        final_qkv_w,
        final_qv_b,
        final_proj_w,
        final_proj_b,
        final_up_w,
        final_up_b,
        final_down_w,
        final_down_b,
    )


def solution(mesh):
    return jax.shard_map(
        shards,
        mesh=mesh,
        in_specs=(
            P(("shard", "rep"), None),
            P(("shard", "rep"), None),
            P("shard", None),
            P("shard"),
            P("shard", None),
            P("shard"),
            P("shard", None),
            P("shard"),
            P("shard", None),
            P("shard"),
            P("shard", None),
            P("shard"),
            P(("shard", "rep"), None),
        ),
        out_specs=(
            P(("shard", "rep"), None),
            P(("shard", "rep"), None),
            P(("shard", "rep"), None),
            P("shard", None),
            P("shard"),
            P("shard", None),
            P("shard"),
            P("shard", None),
            P("shard"),
            P("shard", None),
            P("shard"),
            P("shard", None),
            P("shard"),
        ),
        check_vma=False,
    )
```

```python
import functools

import jax
import jax.numpy as jnp
from jax import lax
from jax.experimental import pallas as pl
from jax.experimental.pallas import tpu as pltpu
from jax.sharding import PartitionSpec as P

HEAD_DIM = 64


EPSILON = 1e-06


def layer_norm(values):
    center = values - jnp.mean(values, axis=-1, keepdims=True)
    spread = jnp.mean(center * center, axis=-1, keepdims=True)
    return center * lax.rsqrt(spread + EPSILON)


def modulate(values, shift_rows, scale_rows):
    return layer_norm(values) * (1.0 + scale_rows[:, None, :]) + shift_rows[:, None, :]


def gelu_tanh(values):
    return jax.nn.gelu(values, approximate=True)


def project(inputs, weight):
    return jnp.einsum("lsd,de->lse", inputs, weight, preferred_element_type=jnp.float32)


def project_back(gradient, weight):
    return jnp.einsum("lse,de->lsd", gradient, weight, preferred_element_type=jnp.float32)


def weight_grad(inputs, gradient):
    return jnp.einsum("lsd,lse->de", inputs, gradient, preferred_element_type=jnp.float32)


def column_sums(gradient):
    return jnp.sum(gradient, axis=(0, 1), dtype=jnp.float32)


def in_order(pieces, shard_at):
    count = len(pieces)
    doubled = jnp.stack(pieces + pieces)
    return lax.dynamic_slice_in_dim(doubled, count - shard_at, count, axis=0)


def unblock(rows, height):
    return jnp.concatenate(jnp.split(rows, rows.shape[0] // height, axis=0), axis=1)


def block_grad(grad, shard_count):
    rows, columns = grad.shape
    pieces = jnp.split(grad, columns // rows, axis=1)
    return jnp.concatenate([piece.reshape(shard_count, -1, rows) for piece in pieces], axis=1)


def gather_kernel(
    shard_count, rep_count, split_bits, latent_count,
    small_ref, ada_ref, bias_ref, qkv_ref, proj_ref, up_ref, down_ref,
    qkv_out, proj_out, up_out, down_out, small_out, mod_out,
    small_buf, mod_send, mod_came, wide_buf, narrow_buf, send_sems, recv_sems,
):
    shard_at, rep_at = lax.axis_index("shard"), lax.axis_index("rep")
    sides = [lax.rem(rep_at // (1 << at), 2) for at in range(split_bits)]
    peers = [rep_at + (1 << at) - 2 * (1 << at) * sides[at] for at in range(split_bits)]
    targets = [lax.rem(shard_at + hop, shard_count) for hop in range(shard_count)]
    width = proj_ref.shape[1]
    part = proj_ref.shape[0]

    barrier = pltpu.get_barrier_semaphore()
    partners = [{"rep": peer} for peer in peers] + [{"shard": at} for at in targets[1:]]
    for partner in partners:
        pl.semaphore_signal(
            barrier, inc=1, device_id=partner, device_id_type=pl.DeviceIdType.MESH
        )
    small_buf[0] = small_ref[...]
    for at in range(qkv_ref.shape[1] // width):
        narrow_buf[shard_at, at * part : (at + 1) * part] = qkv_ref[:, at * width : (at + 1) * width]
    qkv_rows = part * (qkv_ref.shape[1] // width)
    narrow_buf[shard_at, qkv_rows : qkv_rows + part] = proj_ref[...]
    up_groups = up_ref.shape[1] // width
    for at in range(up_groups):
        wide_buf[shard_at, at * part : (at + 1) * part] = up_ref[:, at * width : (at + 1) * width]
    down_rows = down_ref.shape[0]
    wide_buf[shard_at, up_groups * part : up_groups * part + down_rows] = down_ref[...]
    pl.semaphore_wait(barrier, len(partners))
    used = [0]

    def send(source, landing, partner):
        at = used[0]
        used[0] += 1
        copy = pltpu.make_async_remote_copy(
            src_ref=source,
            dst_ref=landing,
            send_sem=send_sems.at[at],
            recv_sem=recv_sems.at[at],
            device_id=partner,
            device_id_type=pl.DeviceIdType.MESH,
        )
        copy.start()
        return copy

    def mod_steps():
        copies = [
            send(small_buf.at[0], small_buf.at[shard_count - hop], {"shard": targets[hop]})
            for hop in range(1, shard_count)
        ]
        yield
        for copy in copies:
            copy.wait()
        copies = []
        for near in list(range(1, shard_count)) + [0]:
            cond = small_buf[near][:latent_count]
            silu_low = (cond / (1.0 + jnp.exp(-cond))).astype(jnp.bfloat16)
            mod_send[near] = (
                jnp.dot(silu_low, ada_ref[...], preferred_element_type=jnp.float32)
                + bias_ref[...]
            )
            if near > 0:
                copies.append(
                    send(mod_send.at[near], mod_came.at[near - 1], {"shard": targets[near]})
                )
        yield
        total = mod_send[0]
        for copy in copies:
            copy.wait()
        for near in range(1, shard_count):
            total = total + mod_came[near - 1]
        mod_out[...] = total
        small_out[...] = small_buf[...]

    def weight_steps(buffer, order):
        rows = buffer.shape[1] >> split_bits
        place = 0
        for level, at in enumerate(order):
            place = place + sides[at] * (1 << level)
        start = pl.multiple_of(place * rows, 16)
        piece = buffer.at[shard_at, pl.ds(start, rows)]
        copies = [
            send(piece, piece, {"shard": targets[hop]}) for hop in range(1, shard_count)
        ]
        yield
        for copy in copies:
            copy.wait()
        for level, at in enumerate(order):
            copies = []
            for hop in range(1, shard_count):
                piece = buffer.at[targets[hop], pl.ds(pl.multiple_of(place * rows, 16), rows << level)]
                copies.append(send(piece, piece, {"rep": peers[at]}))
            yield
            for copy in copies:
                copy.wait()
            place = place - sides[at] * (1 << level)

    order = list(range(split_bits))[::-1]
    other = order[:-1][::-1] + order[-1:]
    running = [mod_steps(), weight_steps(narrow_buf, other), weight_steps(wide_buf, order)]
    while running:
        running = [steps for steps in running if next(steps, "end") is None]
    for owner in range(shard_count):
        into = slice(owner * part, (owner + 1) * part)
        for at in range(qkv_ref.shape[1] // width):
            qkv_out[into, at * width : (at + 1) * width] = narrow_buf[
                owner, at * part : (at + 1) * part
            ]
        proj_out[into, :] = narrow_buf[owner, qkv_rows : qkv_rows + part]
        for at in range(up_groups):
            up_out[into, at * width : (at + 1) * width] = wide_buf[
                owner, at * part : (at + 1) * part
            ]
        down_out[owner * down_rows : (owner + 1) * down_rows, :] = wide_buf[
            owner, up_groups * part : up_groups * part + down_rows
        ]


def gather_all(
    small, ada_wide, wide_bias, qkv_weight, proj_weight, up_weight, down_weight,
    shard_count, rep_count, latent_count,
):
    split_bits = min(rep_count.bit_length() - 1, 3)
    width, mod_width = proj_weight.shape[1], ada_wide.shape[1]
    wide_rows = up_weight.shape[0] * (up_weight.shape[1] // width) + down_weight.shape[0]
    narrow_rows = qkv_weight.shape[0] * (qkv_weight.shape[1] // width) + proj_weight.shape[0]
    copies = 2 * shard_count + 2 * shard_count * (split_bits + 1)
    outs = [
        jax.ShapeDtypeStruct((weight.shape[0] * shard_count, weight.shape[1]), jnp.bfloat16)
        for weight in (qkv_weight, proj_weight, up_weight, down_weight)
    ]
    outs += [
        jax.ShapeDtypeStruct((shard_count,) + small.shape, jnp.float32),
        jax.ShapeDtypeStruct((latent_count, mod_width), jnp.float32),
    ]
    return pl.pallas_call(
        functools.partial(gather_kernel, shard_count, rep_count, split_bits, latent_count),
        out_shape=outs,
        in_specs=[pl.BlockSpec(memory_space=pltpu.VMEM)] * 7,
        out_specs=[pl.BlockSpec(memory_space=pltpu.VMEM)] * len(outs),
        scratch_shapes=[
            pltpu.VMEM((shard_count,) + small.shape, jnp.float32),
            pltpu.VMEM((shard_count, latent_count, mod_width), jnp.float32),
            pltpu.VMEM((shard_count - 1, latent_count, mod_width), jnp.float32),
            pltpu.VMEM((shard_count, wide_rows, width), jnp.bfloat16),
            pltpu.VMEM((shard_count, narrow_rows, width), jnp.bfloat16),
            pltpu.SemaphoreType.DMA((copies,)),
            pltpu.SemaphoreType.DMA((copies,)),
        ],
        compiler_params=pltpu.CompilerParams(
            collective_id=1, has_side_effects=True, vmem_limit_bytes=56 * 1024 * 1024
        ),
    )(small, ada_wide, wide_bias, qkv_weight, proj_weight, up_weight, down_weight)


def reduce_kernel(
    shard_count, rep_count, plans, half_mod, lane_total, *refs
):
    refs = list(refs)
    lane_refs = [refs.pop(0) for _ in range(lane_total)]
    small_ref, mod_ref, ada_ref = refs.pop(0), refs.pop(0), refs.pop(0)
    lane_outs = [refs.pop(0) for _ in range(lane_total)]
    small_out, mod_out, cond_out = refs.pop(0), refs.pop(0), refs.pop(0)
    bits_total = rep_count.bit_length() - 1
    lane_bufs = []
    for _ in range(lane_total):
        stages = [[refs.pop(0) for _ in range(3)] for _ in range(bits_total)]
        lane_bufs.append((stages, refs.pop(0), refs.pop(0), refs.pop(0)))
    small_acc, small_came, small_z = refs.pop(0), refs.pop(0), refs.pop(0)
    mod_buf, cond_send, cond_came = refs.pop(0), refs.pop(0), refs.pop(0)
    send_sems, recv_sems = refs
    shard_at, rep_at = lax.axis_index("shard"), lax.axis_index("rep")
    bits = [1 << i for i in range(bits_total)]
    sides = [lax.rem(rep_at // bit, 2) for bit in bits]
    peers = [rep_at + bit - 2 * bit * side for bit, side in zip(bits, sides)]
    targets = [lax.rem(shard_at + hop, shard_count) for hop in range(shard_count)]

    barrier = pltpu.get_barrier_semaphore()
    partners = [{"rep": peer} for peer in peers] + [{"shard": at} for at in targets[1:]]
    for partner in partners:
        pl.semaphore_signal(
            barrier, inc=1, device_id=partner, device_id_type=pl.DeviceIdType.MESH
        )
    pl.semaphore_wait(barrier, len(partners))
    used = [0]

    def send(source, landing, partner):
        at = used[0]
        used[0] += 1
        copy = pltpu.make_async_remote_copy(
            src_ref=source,
            dst_ref=landing,
            send_sem=send_sems.at[at],
            recv_sem=recv_sems.at[at],
            device_id=partner,
            device_id_type=pl.DeviceIdType.MESH,
        )
        copy.start()
        return copy

    def lane_steps(lane):
        (order, halved), source = plans[lane], lane_refs[lane]
        stages, z_send, z_came, final = lane_bufs[lane]
        offset = 0
        for at, split, (sent, came, kept) in zip(order, halved, stages):
            rows = sent.shape[1]
            side = sides[at]
            if split:
                away = pl.multiple_of((1 - side) * rows, 16)
                stay = pl.multiple_of(side * rows, 16)
                sent[...] = source[:, pl.ds(away, rows), :].astype(jnp.bfloat16)
            else:
                sent[...] = source[...].astype(jnp.bfloat16)
            copy = send(sent, came, {"rep": peers[at]})
            yield
            copy.wait()
            if split:
                kept[...] = source[:, pl.ds(stay, rows), :] + came[...].astype(jnp.float32)
                offset = offset + side * rows
            else:
                kept[...] = sent[...].astype(jnp.float32) + came[...].astype(jnp.float32)
            source = kept
        z_send[...] = source[...].astype(jnp.bfloat16)
        copies = [
            send(z_send.at[targets[hop]], z_came.at[hop - 1], {"shard": targets[hop]})
            for hop in range(1, shard_count)
        ]
        yield
        total = source[shard_at]
        for copy in copies:
            copy.wait()
        for hop in range(1, shard_count):
            total = total + z_came[hop - 1].astype(jnp.float32)
        rows = total.shape[0]
        final[pl.ds(pl.multiple_of(offset, 16), rows), :] = total.astype(jnp.bfloat16)
        for at, split in list(zip(order, halved))[::-1]:
            if not split:
                continue
            place = final.at[pl.ds(pl.multiple_of(offset, 16), rows), :]
            copy = send(place, place, {"rep": peers[at]})
            yield
            copy.wait()
            offset = offset - sides[at] * rows
            rows = rows * 2
        lane_outs[lane][...] = final[...].astype(jnp.float32)

    def small_steps():
        small_acc[0] = small_ref[...]
        for at in range(bits_total):
            copy = send(small_acc.at[at], small_came.at[at], {"rep": peers[at]})
            yield
            copy.wait()
            small_acc[at + 1] = small_acc[at] + small_came[at]
        copies = [
            send(
                small_acc.at[bits_total, targets[hop]],
                small_z.at[hop - 1],
                {"shard": targets[hop]},
            )
            for hop in range(1, shard_count)
        ]
        yield
        total = small_acc[bits_total, shard_at]
        for copy in copies:
            copy.wait()
        for hop in range(1, shard_count):
            total = total + small_z[hop - 1]
        small_out[...] = total

    def mod_steps():
        mod_buf[0] = mod_ref[...]
        copies = [
            send(mod_buf.at[0], mod_buf.at[shard_count - hop], {"shard": targets[hop]})
            for hop in range(1, shard_count)
        ]
        yield
        for copy in copies:
            copy.wait()
        filled = shard_count
        copy = None
        cond_copies = []
        for at in range(bits_total)[::-1]:
            copy = send(
                mod_buf.at[pl.ds(0, filled)], mod_buf.at[pl.ds(filled, filled)], {"rep": peers[at]}
            )
            if filled == shard_count:
                for near in range(shard_count):
                    rows = mod_buf[near][:, :half_mod]
                    dims = (((1,), (1,)), ((), ()))
                    first = lax.dot_general(
                        rows, ada_ref[:, :half_mod], dims, preferred_element_type=jnp.float32
                    )
                    second = lax.dot_general(
                        rows, ada_ref[:, half_mod:], dims, preferred_element_type=jnp.float32
                    )
                    lat = rows.shape[0] // 2
                    cond_send[near] = first[:lat] + second[lat:]
                cond_copies = [
                    send(cond_send.at[hop], cond_came.at[hop - 1], {"shard": targets[hop]})
                    for hop in range(1, shard_count)
                ]
            yield
            copy.wait()
            filled = filled * 2
        for done in cond_copies:
            done.wait()
        cond_out[0] = cond_send[0]
        for hop in range(1, shard_count):
            cond_out[hop] = cond_came[hop - 1]
        mod_out[...] = mod_buf[...]

    running = [lane_steps(lane) for lane in range(lane_total)] + [mod_steps(), small_steps()]
    while running:
        running = [steps for steps in running if next(steps, "end") is None]


def reduce_all(lanes, small, mod_slot, ada_padded, shard_count, rep_count, half_mod):
    bits_total = rep_count.bit_length() - 1
    plans, scratch, outs = [], [], []
    copies = 0
    for at, lane in enumerate(lanes):
        count, rows, width = lane.shape
        order = list(range(bits_total))
        if at % 2 == 1:
            order = order[:1] + order[:0:-1]
        halved = []
        for _ in order:
            split = rows % 32 == 0
            halved.append(split)
            rows = rows // 2 if split else rows
            scratch.append(pltpu.VMEM((count, rows, width), jnp.bfloat16))
            scratch.append(pltpu.VMEM((count, rows, width), jnp.bfloat16))
            scratch.append(pltpu.VMEM((count, rows, width), jnp.float32))
        scratch.append(pltpu.VMEM((count, rows, width), jnp.bfloat16))
        scratch.append(pltpu.VMEM((count - 1, rows, width), jnp.bfloat16))
        scratch.append(pltpu.VMEM((lane.shape[1], width), jnp.bfloat16))
        plans.append((order, halved))
        outs.append(jax.ShapeDtypeStruct((lane.shape[1], width), jnp.float32))
        copies += 2 * bits_total + shard_count
    slots = shard_count * rep_count
    lat = mod_slot.shape[0] // 2
    scratch += [
        pltpu.VMEM((bits_total + 1,) + small.shape, jnp.float32),
        pltpu.VMEM((bits_total,) + small.shape, jnp.float32),
        pltpu.VMEM((shard_count - 1,) + small.shape[1:], jnp.float32),
        pltpu.VMEM((slots,) + mod_slot.shape, jnp.bfloat16),
        pltpu.VMEM((shard_count, lat, 128), jnp.float32),
        pltpu.VMEM((shard_count - 1, lat, 128), jnp.float32),
    ]
    copies += 2 * bits_total + 3 * shard_count
    scratch += [pltpu.SemaphoreType.DMA((copies,)), pltpu.SemaphoreType.DMA((copies,))]
    outs += [
        jax.ShapeDtypeStruct(small.shape[1:], jnp.float32),
        jax.ShapeDtypeStruct((slots,) + mod_slot.shape, jnp.bfloat16),
        jax.ShapeDtypeStruct((shard_count, lat, 128), jnp.float32),
    ]
    return pl.pallas_call(
        functools.partial(reduce_kernel, shard_count, rep_count, plans, half_mod, len(lanes)),
        out_shape=outs,
        in_specs=[pl.BlockSpec(memory_space=pltpu.VMEM)] * (len(lanes) + 3),
        out_specs=[pl.BlockSpec(memory_space=pltpu.VMEM)] * len(outs),
        scratch_shapes=scratch,
        compiler_params=pltpu.CompilerParams(
            collective_id=0, has_side_effects=True, vmem_limit_bytes=56 * 1024 * 1024
        ),
    )(*lanes, small, mod_slot, ada_padded)


def shards(
    latents_in,
    conditioning,
    ada_weight,
    ada_bias,
    qkv_weight,
    qv_bias,
    proj_weight,
    proj_bias,
    fc1_weight,
    fc1_bias,
    fc2_weight,
    fc2_bias,
    cotangent,
):
    latent_count = conditioning.shape[0]
    model_width = conditioning.shape[1]
    seq_length = latents_in.shape[0] // latent_count
    head_count = model_width // HEAD_DIM
    softmax_scale = HEAD_DIM ** (-0.5)
    shard_count = lax.axis_size("shard")
    rep_count = lax.axis_size("rep")
    shard_at = lax.axis_index("shard")
    rep_at = lax.axis_index("rep")
    part = model_width // shard_count
    small_rows = jnp.concatenate([qv_bias, proj_bias, fc1_bias, fc2_bias])
    small_rows = small_rows.reshape(-1, model_width)
    padded = jnp.pad(
        jnp.concatenate([conditioning, small_rows], axis=0).astype(jnp.float32),
        ((0, 16 - latent_count - small_rows.shape[0]), (0, 0)),
    )
    ada_wide = lax.dynamic_update_slice_in_dim(
        jnp.zeros((model_width, ada_weight.shape[1]), jnp.bfloat16), ada_weight,
        shard_at * part, axis=0,
    )
    wide_bias = lax.dynamic_update_slice_in_dim(
        jnp.zeros((1, ada_weight.shape[1]), jnp.float32), ada_bias.astype(jnp.float32)[None],
        shard_at * ada_bias.shape[0], axis=1,
    )
    qkv_matrix, proj_matrix, up_matrix, down_matrix, small_near, modulation = gather_all(
        padded, ada_wide, wide_bias, qkv_weight, proj_weight, fc1_weight, fc2_weight,
        shard_count, rep_count, latent_count,
    )
    small_end = latent_count + small_rows.shape[0]
    small_all = in_order([small_near[i, latent_count:small_end] for i in range(shard_count)], shard_at)
    small_all = small_all.astype(jnp.bfloat16)
    small_all = small_all.reshape(shard_count, -1)
    edges = [0]
    for vector in (qv_bias, proj_bias, fc1_bias, fc2_bias):
        edges.append(edges[-1] + vector.shape[0])
    qv_offsets, proj_offsets, up_offsets, down_offsets = (
        small_all[:, edges[i] : edges[i + 1]].reshape(-1) for i in range(4)
    )
    inputs = latents_in.astype(jnp.float32).reshape(latent_count, seq_length, model_width)
    _, silu_pull = jax.vjp(jax.nn.silu, conditioning.astype(jnp.float32))
    shift_one, scale_one, gate_one, shift_two, scale_two, gate_two = jnp.split(
        modulation, 6, axis=1
    )
    first_in, first_pull = jax.vjp(modulate, inputs, shift_one, scale_one)
    first_low = first_in.astype(jnp.bfloat16)
    zero_bias = jnp.zeros((model_width,), jnp.bfloat16)
    full_bias = jnp.concatenate(
        [qv_offsets[:model_width], zero_bias, qv_offsets[model_width:]]
    ).astype(jnp.float32)
    qkv_low = (project(first_low, qkv_matrix) + full_bias).astype(jnp.bfloat16)
    qkv_low = qkv_low.reshape(latent_count, seq_length, 3, head_count, HEAD_DIM)
    queries = qkv_low[:, :, 0]
    key_rows = qkv_low[:, :, 1]
    value_rows = qkv_low[:, :, 2]
    scores = (
        jnp.einsum("lqhd,lkhd->lhqk", queries, key_rows, preferred_element_type=jnp.float32)
        * softmax_scale
    )
    row_max = jnp.max(scores, axis=-1, keepdims=True)
    log_total = row_max + jnp.log(jnp.sum(jnp.exp(scores - row_max), axis=-1, keepdims=True))
    probs_fwd = jnp.exp(scores - log_total).astype(jnp.bfloat16)
    attended = jnp.einsum(
        "lhqk,lkhd->lqhd", probs_fwd, value_rows, preferred_element_type=jnp.float32
    )
    attended_low = attended.reshape(latent_count, seq_length, model_width).astype(jnp.bfloat16)
    attn_out = project(attended_low, proj_matrix) + proj_offsets.astype(jnp.float32)
    middle = inputs + gate_one[:, None, :] * attn_out
    second_in, second_pull = jax.vjp(modulate, middle, shift_two, scale_two)
    second_low = second_in.astype(jnp.bfloat16)
    hidden_pre = project(second_low, up_matrix) + up_offsets.astype(jnp.float32)
    hidden_act, gelu_pull = jax.vjp(gelu_tanh, hidden_pre)
    hidden_low = hidden_act.astype(jnp.bfloat16)
    branch_out = project(hidden_low, down_matrix) + down_offsets.astype(jnp.float32)
    result = middle + gate_two[:, None, :] * branch_out
    upstream = cotangent.astype(jnp.float32).reshape(latent_count, seq_length, model_width)
    down_grad = (gate_two[:, None, :] * upstream).astype(jnp.bfloat16)
    gate_two_grad = jnp.sum(upstream * branch_out, axis=1)
    down_w_grad = weight_grad(hidden_low, down_grad)
    down_b_grad = column_sums(down_grad)
    hidden_grad = gelu_pull(project_back(down_grad, down_matrix))[0].astype(jnp.bfloat16)
    up_w_grad = weight_grad(second_low, hidden_grad)
    up_b_grad = column_sums(hidden_grad)
    middle_part, shift_two_grad, scale_two_grad = second_pull(project_back(hidden_grad, up_matrix))
    middle_grad = upstream + middle_part
    attn_grad = (gate_one[:, None, :] * middle_grad).astype(jnp.bfloat16)
    gate_one_grad = jnp.sum(middle_grad * attn_out, axis=1)
    proj_w_grad = weight_grad(attended_low, attn_grad)
    proj_b_grad = column_sums(attn_grad)
    attended_grad = project_back(attn_grad, proj_matrix).astype(jnp.bfloat16)
    attended_grad = attended_grad.reshape(latent_count, seq_length, head_count, HEAD_DIM)
    scores_again = (
        jnp.einsum("lqhd,lkhd->lhqk", queries, key_rows, preferred_element_type=jnp.float32)
        * softmax_scale
    )
    probs_again = jnp.exp(scores_again - log_total)
    value_grad = jnp.einsum(
        "lhqk,lqhd->lkhd",
        probs_again.astype(jnp.bfloat16),
        attended_grad,
        preferred_element_type=jnp.float32,
    )
    probs_grad = jnp.einsum(
        "lqhd,lkhd->lhqk", attended_grad, value_rows, preferred_element_type=jnp.float32
    )
    score_grad = probs_again * (
        probs_grad - jnp.sum(probs_again * probs_grad, axis=-1, keepdims=True)
    )
    score_low = score_grad.astype(jnp.bfloat16)
    query_grad = (
        jnp.einsum("lhqk,lkhd->lqhd", score_low, key_rows, preferred_element_type=jnp.float32)
        * softmax_scale
    )
    key_grad = (
        jnp.einsum("lhqk,lqhd->lkhd", score_low, queries, preferred_element_type=jnp.float32)
        * softmax_scale
    )
    qkv_grad = jnp.stack([query_grad, key_grad, value_grad], axis=2)
    qkv_grad = qkv_grad.reshape(latent_count, seq_length, 3 * model_width).astype(jnp.bfloat16)
    qkv_w_grad = weight_grad(first_low, qkv_grad)
    qkv_sums = column_sums(qkv_grad)
    qv_b_grad = jnp.concatenate([qkv_sums[:model_width], qkv_sums[2 * model_width :]])
    input_part, shift_one_grad, scale_one_grad = first_pull(project_back(qkv_grad, qkv_matrix))
    input_grad = middle_grad + input_part
    mod_grad = jnp.concatenate(
        [
            shift_one_grad,
            scale_one_grad,
            gate_one_grad,
            shift_two_grad,
            scale_two_grad,
            gate_two_grad,
        ],
        axis=1,
    ).astype(jnp.bfloat16)
    late = jnp.concatenate(
        [proj_w_grad.reshape(shard_count, -1, model_width), block_grad(qkv_w_grad, shard_count)],
        axis=1,
    )
    lanes = (
        down_w_grad.reshape(shard_count, -1, model_width),
        block_grad(up_w_grad, shard_count),
        late,
    )
    small_grads = jnp.concatenate(
        [
            vector.reshape(shard_count, -1)
            for vector in (qv_b_grad, proj_b_grad, up_b_grad, down_b_grad)
        ],
        axis=1,
    )
    small_width = small_grads.shape[1]
    small_grads = jnp.pad(small_grads, ((0, 0), (0, 1024 - small_width)))
    half_mod, half_silu = mod_grad.shape[1] // 2, model_width // 2
    silu_mid = jax.nn.silu(conditioning.astype(jnp.float32)).astype(jnp.bfloat16)
    silu_fold = jnp.concatenate([silu_mid[:, :half_silu], silu_mid[:, half_silu:]], axis=0)
    mod_slot = jnp.concatenate(
        [
            jnp.concatenate([mod_grad[:, :half_mod], mod_grad[:, half_mod:]], axis=0),
            jnp.pad(silu_fold, ((0, 0), (0, 256 - half_silu))),
        ],
        axis=1,
    )
    down_sum, up_sum, late_sum, small_final, mod_slots, cond_near_grad = reduce_all(
        lanes,
        small_grads.reshape(shard_count, 8, 128),
        mod_slot,
        jnp.pad(ada_weight, ((0, 128 - part), (0, 0))),
        shard_count,
        rep_count,
        half_mod,
    )
    small_final = small_final.reshape(-1)
    pieces = [cond_near_grad[i, :, :part] for i in range(shard_count)]
    cond_grad = in_order(pieces[:1] + pieces[:0:-1], shard_at)
    cond_grad = cond_grad.transpose(1, 0, 2).reshape(latent_count, model_width)
    cond_grad = silu_pull(cond_grad)[0]
    top, bottom = mod_slots[:, :latent_count], mod_slots[:, latent_count:]
    mod_all = jnp.concatenate([top[:, :, :half_mod], bottom[:, :, :half_mod]], axis=2)
    mod_all = mod_all.reshape(-1, 2 * half_mod)
    silu_all = jnp.concatenate(
        [
            top[:, :, half_mod : half_mod + half_silu],
            bottom[:, :, half_mod : half_mod + half_silu],
        ],
        axis=2,
    ).reshape(-1, model_width)
    silu_all = lax.dynamic_slice_in_dim(silu_all, shard_at * part, part, axis=1)
    final_ada_w = jnp.einsum("ld,le->de", silu_all, mod_all, preferred_element_type=jnp.float32)
    bias_cols = ada_bias.shape[0]
    final_ada_b = jnp.sum(
        lax.dynamic_slice_in_dim(mod_all, shard_at * bias_cols, bias_cols, axis=1),
        axis=0,
        dtype=jnp.float32,
    )
    final_down_w = down_sum
    final_up_w = unblock(up_sum, part)
    final_proj_w = late_sum[:part]
    final_qkv_w = unblock(late_sum[part:], part)
    final_qv_b, final_proj_b, final_up_b, final_down_b = (
        small_final[edges[i] : edges[i + 1]] for i in range(4)
    )
    return (
        result.reshape(latent_count * seq_length, model_width).astype(jnp.bfloat16),
        input_grad.reshape(latent_count * seq_length, model_width),
        cond_grad,
        final_ada_w,
        final_ada_b,
        final_qkv_w,
        final_qv_b,
        final_proj_w,
        final_proj_b,
        final_up_w,
        final_up_b,
        final_down_w,
        final_down_b,
    )


def solution(mesh):
    return jax.shard_map(
        shards,
        mesh=mesh,
        in_specs=(
            P(("shard", "rep"), None),
            P(("shard", "rep"), None),
            P("shard", None),
            P("shard"),
            P("shard", None),
            P("shard"),
            P("shard", None),
            P("shard"),
            P("shard", None),
            P("shard"),
            P("shard", None),
            P("shard"),
            P(("shard", "rep"), None),
        ),
        out_specs=(
            P(("shard", "rep"), None),
            P(("shard", "rep"), None),
            P(("shard", "rep"), None),
            P("shard", None),
            P("shard"),
            P("shard", None),
            P("shard"),
            P("shard", None),
            P("shard"),
            P("shard", None),
            P("shard"),
            P("shard", None),
            P("shard"),
        ),
        check_vma=False,
    )
```
